128 devices in a mesh: node: 4 (over z_lo, core), dp: 32 (over z_hi, x, y).
Axes of the slice: x: 4, y: 4, z: 4 (z_hi: 2, z_lo: 2; z = z_hi * 2 + z_lo), core: 2. Of those that a mesh axis runs over, the one named last changes fastest.
Arguments:
- tokens: bfloat16 [65536, 4096], P(('node', 'dp')), may hold values from -24 to 24
- cotangent: bfloat16 [65536, 1792], P(('node', 'dp')), may hold values from -6 to 6
- master: float32 [1792, 4096], P('node', 'dp'), may hold values from -3 to 3
- moment_one: float32 [1792, 4096], P('node', 'dp'), may hold values from -6 to 6
- moment_two: float32 [1792, 4096], P('node', 'dp'), may hold values from 0.25 to 4
Outputs:
- outputs: bfloat16 [65536, 1792], P(('node', 'dp'))
- input_grad: bfloat16 [65536, 4096], P(('node', 'dp'))
- new_master: float32 [1792, 4096], P('node', 'dp')
- new_one: float32 [1792, 4096], P('node', 'dp')
- new_two: float32 [1792, 4096], P('node', 'dp')
- new_copy: bfloat16 [1792, 4096], P('node')
The draws below stay inside these ranges and needn't reach their ends.
All inputs are finite; a program needn't handle non-finite values.
Results may differ from the reference program's by a relative error of at most 0.005.
Values may be sent and summed in bfloat16 or wider, within the bound.
A program may use at most 128 MiB of HBM per device.

```python
import math
import jax
import jax.numpy as jnp
from jax import lax

D = 4096
FF = 1792
TOK_DEV = 512
TOKENS = 65536
N_NODE = 4
N_DP = 32


def raised(entries, rng, source, target, blocks, factor):
    def block_of(axis_at):
        return (jnp.arange(entries.shape[axis_at]) // (entries.shape[axis_at] // blocks)).reshape((-1,) + (1,) * (entries.ndim - 1 - axis_at))

    near = jax.random.permutation(rng, blocks)[block_of(target)]
    other_side = (block_of(target) + blocks // 2) % blocks
    return jnp.where((block_of(source) == near) | (block_of(source) == other_side), factor * entries, entries)


def block_scale(own_key, dims, split, least, high):
    def one(position, parts):
        heights = jax.random.uniform(jax.random.fold_in(jax.random.fold_in(own_key, 6), position), (parts,), jnp.float32, least / len(split), high / len(split))
        return jnp.repeat(jnp.exp(heights), dims[position] // parts).reshape((-1,) + (1,) * (len(dims) - position - 1))

    gain = one(*split[0])
    for cut in split[1:]:
        gain = gain * one(*cut)
    return gain


def gaussian(stream_key, shape, spread, reach, pieces=(), held_as=jnp.bfloat16):
    loudness = block_scale(stream_key, shape, pieces, -0.22, 0.18) if pieces else 1.0
    drawn = jax.random.normal(stream_key, shape, jnp.float32) * spread * loudness
    return jnp.minimum(jnp.maximum(drawn, -reach), reach).astype(held_as)


def bell_draw_with(own_key, dims, deviation, bound, pieces, heavy, kind=jnp.bfloat16):
    result = deviation * jax.random.normal(own_key, dims, jnp.float32)
    if pieces:
        result = result * block_scale(own_key, dims, pieces, -0.22, 0.18)
    return jnp.clip(raised(result, jax.random.fold_in(own_key, 3), *heavy), -bound, bound).astype(kind)


def setup_inputs(seed: int = 0) -> dict:
    key_list = jax.random.split(jax.random.key(seed), 6)
    return {
        "tokens": bell_draw_with(key_list[0], (TOKENS, D), 1.0, 24.0, ((0, 128),), (0, 1, 128, 5.5)),
        "cotangent": gaussian(key_list[1], (TOKENS, FF), 1.0, 6.0, ((0, 128),)),
        "master": gaussian(key_list[2], (FF, D), 0.5, 3.0, ((0, 4), (1, 32)), jnp.float32),
        "moment_one": gaussian(key_list[3], (FF, D), 1.0, 6.0, ((0, 4), (1, 32)), jnp.float32),
        "moment_two": jnp.clip(jnp.exp(math.log(4.0) - 2.7725887 * jax.random.uniform(key_list[4], (FF, D), jnp.float32) ** block_scale(key_list[4], (FF, D), ((0, 4), (1, 32)), -0.2, 0.2)), 0.25, 4.0),
    }


beta_one = 0.9
beta_two = 0.95
epsilon = 1e-08
step_size = 0.2
decay_rate = 0.1
step_count = 10

def reference(tokens, cotangent, master, moment_one, moment_two):
    working = master.astype(jnp.bfloat16)
    width = tokens.shape[1]
    hidden = cotangent.shape[1]
    forward = lax.dot_general(tokens, working, (((1,), (1,)), ((), ())), preferred_element_type=jnp.float32)
    outputs = (forward / math.sqrt(width)).astype(jnp.bfloat16)
    backward = jnp.dot(cotangent, working, preferred_element_type=jnp.float32)
    input_grad = (backward / math.sqrt(hidden)).astype(jnp.bfloat16)
    blocks = N_NODE * N_DP
    token_blocks = tokens.reshape(blocks, TOK_DEV, width)
    grad_blocks = cotangent.reshape(blocks, TOK_DEV, hidden)

    def accumulate(total, pair):
        token_part, grad_part = pair
        term = lax.dot_general(grad_part, token_part, (((0,), (0,)), ((), ())), preferred_element_type=jnp.float32)
        rounded = lax.optimization_barrier(term.astype(jnp.bfloat16))
        return (total + rounded.astype(jnp.float32), None)
    weight_sum, _ = lax.scan(accumulate, jnp.zeros((hidden, width), jnp.float32), (token_blocks, grad_blocks))
    grad = weight_sum / math.sqrt(TOKENS)
    new_one = beta_one * moment_one + (1.0 - beta_one) * grad
    new_two = beta_two * moment_two + (1.0 - beta_two) * grad * grad
    first_fix = 1.0 - beta_one ** step_count
    second_fix = 1.0 - beta_two ** step_count
    update = new_one / first_fix / (jnp.sqrt(new_two / second_fix) + epsilon)
    new_master = master - step_size * (update + decay_rate * master)
    new_copy = new_master.astype(jnp.bfloat16)
    return (outputs, input_grad, new_master, new_one, new_two, new_copy)
```

```python
import math

import jax
import jax.numpy as jnp
from jax import lax
from jax.experimental import pallas as pl
from jax.experimental.pallas import tpu as pltpu
from jax.sharding import PartitionSpec as P

beta_one = 0.9
beta_two = 0.95
epsilon = 1e-08
step_size = 0.2
decay_rate = 0.1
step_count = 10

MESH = pl.DeviceIdType.MESH
AXES = ("z", "x", "y")
BF = jnp.bfloat16
F32 = jnp.float32

ROWS = 448
PAD = 512
LANE = 128
TOK = 512
CHUNK = 512
N_CHUNK = 8
PARTS = ((0, 192, "xyz"), (192, 128, "yzx"), (320, 128, "zxy"))
COPY_PARTS = ((0, 224, "xy"), (224, 224, "yx"))


def device_at(co):
    return (
        lax.rem(co["z"], 2) * 2 + co["c"],
        lax.div(co["z"], 2) * 16 + co["x"] * 4 + co["y"],
    )


def moved(co, axis, by):
    other = dict(co)
    other[axis] = lax.rem(co[axis] + by + 4, 4)
    return other


def kernel(
    tokens, cotangent, master, moment_one, moment_two,
    outputs, input_grad, new_master, new_one, new_two, copies,
    tok, cot, cot_t, weights, terms,
    got1a, got1b, got1c, got2a, got2b, got2c, got3a, got3b, got3c,
    grad_sum, out_acc, ig_own, ig_send, ig_recv, out_send, out_recv, out_full,
    state, state_new, copy_own,
    load_sem, tok_sem, ig_out_sem,
    core_send, core_recv, ag_send, ag_recv, rs_send, rs_recv, nc_send, nc_recv,
):
    node = lax.axis_index("node")
    dp = lax.axis_index("dp")
    c = lax.rem(node, 2)
    z_lo = lax.div(node, 2)
    z_hi = lax.div(dp, 16)
    me = {
        "z": z_hi * 2 + z_lo,
        "x": lax.rem(lax.div(dp, 4), 4),
        "y": lax.rem(dp, 4),
        "c": c,
    }
    sibling = device_at({**me, "c": 1 - c})
    opposite_z = device_at(moved(me, "z", 2))
    window = [pl.multiple_of(lo * 896 + c * 384, 128) for lo in range(2)]
    sib_window = [pl.multiple_of(lo * 896 + (1 - c) * 384, 128) for lo in range(2)]
    offset = c * 64

    def remote(src, dst, send, recv, to):
        return pltpu.make_async_remote_copy(
            src_ref=src, dst_ref=dst, send_sem=send, recv_sem=recv,
            device_id=to, device_id_type=MESH,
        )

    def push(src, dst, send, recv, to):
        remote(src, dst, send, recv, to).start()

    def left(src, send, recv):
        remote(src, src, send, recv, sibling).wait_send()

    def arrive(dst, send, recv):
        remote(dst, dst, send, recv, sibling).wait_recv()

    def load_state(k):
        return pltpu.make_async_copy(
            (master, moment_one, moment_two)[k], state.at[k], load_sem.at[k]
        )

    def load_cot(lo):
        return pltpu.make_async_copy(
            cotangent.at[:, pl.ds(window[lo], PAD)],
            cot.at[lo, pl.ds(0, TOK)],
            load_sem.at[3 + lo],
        )

    def chunk_of(i):
        hi = lax.rem(z_hi + 1 - lax.div(i, 4) + 2, 2)
        return hi, lax.rem(me["x"] + 2 + i, 4)

    def columns(q):
        return pl.ds(pl.multiple_of(q * CHUNK, CHUNK), CHUNK)

    def load_tok(i):
        hi, x = chunk_of(i)
        q = hi * 4 + x
        return pltpu.make_async_copy(
            tokens.at[:, columns(q)], tok.at[q, pl.ds(0, TOK)], tok_sem.at[i]
        )

    load_state(0).start()
    load_cot(0).start()
    load_cot(1).start()
    for i in range(N_CHUNK):
        load_tok(i).start()
    load_state(1).start()
    load_state(2).start()

    barrier = pltpu.get_barrier_semaphore()
    peers = [sibling, opposite_z]
    for axis in AXES:
        peers += [device_at(moved(me, axis, 1)), device_at(moved(me, axis, -1))]
    for peer in peers:
        pl.semaphore_signal(barrier, inc=1, device_id=peer, device_id_type=MESH)
    pl.semaphore_wait(barrier, len(peers))

    def rows_of(buffer, first, count):
        if buffer is weights:
            return pl.ds(pl.multiple_of(offset + first, 32), count)
        return pl.ds(first, count)

    class Gather:
        def __init__(self, buffer, names, axis, full, half_axis, first, count, send, recv, base):
            self.buffer, self.names, self.axis, self.full = buffer, names, axis, full
            self.half_axis, self.first, self.count = half_axis, first, count
            self.send, self.recv, self.base = send, recv, base

        def at(self, where, half):
            index = []
            first, count = self.first, self.count
            if self.half_axis is None:
                count = count // 2
                first = first + half * count
            for name in self.names:
                if name == self.half_axis:
                    index.append(pl.ds(half * self.size(name) // 2, self.size(name) // 2))
                elif name == self.axis:
                    index.append(lax.rem(me[name] + where + 4, 4))
                elif name in self.full:
                    index.append(slice(None))
                else:
                    index.append(me[name])
            return self.buffer.at[tuple(index) + (rows_of(self.buffer, first, count), slice(None))]

        def size(self, name):
            return 2 if name == "h" else 4

        def sems(self, way, message):
            k = self.base + way * 3 + message
            return self.send.at[k], self.recv.at[k]

        def start(self):
            for message in range(2):
                for way in range(2):
                    half = message if way == 0 else 1 - message
                    ref = self.at(0, half)
                    push(ref, ref, *self.sems(way, message), device_at(moved(me, self.axis, 1 - 2 * way)))

        def forward(self):
            for way in range(2):
                half = way
                ref = self.at(2 * way - 1, half)
                arrive(ref, *self.sems(way, 0))
                push(ref, ref, *self.sems(way, 2), device_at(moved(me, self.axis, 1 - 2 * way)))

        def finish(self):
            for way in range(2):
                arrive(self.at(2 * way - 1, 1 - way), *self.sems(way, 1))
                arrive(self.at(2, way), *self.sems(way, 2))

        def close(self):
            for way in range(2):
                for message in range(3):
                    left(self.at(0, 0), *self.sems(way, message))

    ag = []
    for p, (first, count, order) in enumerate(PARTS):
        ag.append([
            Gather(
                weights, AXES, order[k], order[:k], order[0] if k else None, first, count,
                ag_send, ag_recv, (p * 3 + k) * 6,
            )
            for k in range(3)
        ])

    nc = []
    for p, (first, count, order) in enumerate(COPY_PARTS):
        nc.append([
            Gather(
                copies, ("h", "x", "y"), order[k], order[:k], "h", first, count,
                nc_send, nc_recv, 2 + (p * 2 + k) * 6,
            )
            for k in range(2)
        ])

    class Reduce:
        def __init__(self, order, stage, first, count, got, base):
            self.order, self.stage, self.first, self.count = order, stage, first, count
            self.axis = order[stage]
            self.got, self.base = got, base

        def index(self, where, half, j=None):
            first, count = self.first, self.count
            if self.stage == 2:
                count = count // 2
                first = first + half * count
            out = []
            for name in AXES:
                k = self.order.index(name)
                if k < self.stage:
                    out.append(me[name])
                elif k == self.stage:
                    out.append(lax.rem(me[name] + where + 4, 4))
                elif k == 2:
                    out.append(pl.ds(2 * half, 2) if j is None else 2 * half + lax.rem(j, 2))
                else:
                    out.append(slice(None) if j is None else lax.div(j, 2))
            return tuple(out) + (pl.ds(first, count), slice(None))

        def got_index(self, slot, j):
            if self.stage == 0:
                names = [n for n in AXES if n != self.axis]
                return (slot,) + tuple(
                    lax.rem(j, 2) if self.order.index(n) == 2 else lax.div(j, 2) for n in names
                )
            if self.stage == 1:
                return (slot, j)
            return (slot,)

        def blocks(self):
            return (8, 2, 1)[self.stage]

        def sems(self, slot):
            return rs_send.at[self.base + slot], rs_recv.at[self.base + slot]

        def out(self, where, half, slot, way):
            push(
                terms.at[self.index(where, half)], self.got.at[slot], *self.sems(slot),
                device_at(moved(me, self.axis, 1 - 2 * way)),
            )

        def start_far(self):
            self.out(2, 0, 0, 0)
            self.out(2, 1, 1, 1)

        def start_near(self, way):
            if way == 0:
                self.out(1, 1, 3, 0)
            else:
                self.out(-1, 0, 5, 1)

        def combine(self):
            for way in range(2):
                arrive(self.got.at[way], *self.sems(way))
                where = 1 - 2 * way

                def add(j, _, way=way, where=where):
                    at = self.index(where, way, j)
                    total = terms[at].astype(F32) + self.got[self.got_index(way, j)].astype(F32)
                    terms[at] = total.astype(BF)
                    return 0

                lax.fori_loop(0, self.blocks(), add, 0)
                self.out(where, way, 2 if way == 0 else 4, way)

        def finish(self):
            for slot in range(2, 6):
                arrive(self.got.at[slot], *self.sems(slot))
            for half, (one, two) in enumerate(((2, 5), (3, 4))):

                def add(j, _, half=half, one=one, two=two):
                    at = self.index(0, half, j)
                    total = (
                        terms[at].astype(F32)
                        + self.got[self.got_index(one, j)].astype(F32)
                        + self.got[self.got_index(two, j)].astype(F32)
                    )
                    if self.stage == 2:
                        size = self.count // 2
                        grad_sum[pl.ds(self.first + half * size, size), :] = total
                    else:
                        terms[at] = total.astype(BF)
                    return 0

                lax.fori_loop(0, self.blocks(), add, 0)

        def close(self):
            for slot in range(6):
                left(self.got.at[slot], *self.sems(slot))

    got = ((got1a, got2a, got3a), (got1b, got2b, got3b), (got1c, got2c, got3c))
    rs = [
        [
            Reduce(order[::-1], k, first, count, got[p][k], (p * 3 + k) * 6)
            for k in range(3)
        ]
        for p, (first, count, order) in enumerate(PARTS)
    ]

    load_state(0).wait()
    weights[me["z"], me["x"], me["y"], pl.ds(pl.multiple_of(offset, 32), ROWS), :] = state[0].astype(BF)
    for p in range(3):
        ag[p][0].start()

    for lo in range(2):
        push(
            cotangent.at[:, pl.ds(sib_window[lo], PAD)], cot.at[lo, pl.ds(TOK, TOK)],
            core_send.at[lo], core_recv.at[lo], sibling,
        )
    for i in range(N_CHUNK):
        hi, x = chunk_of(i)
        q = hi * 4 + x
        push(
            tokens.at[:, columns(q)], tok.at[q, pl.ds(TOK, TOK)],
            core_send.at[2 + i], core_recv.at[2 + i], sibling,
        )

    spare = pl.multiple_of((1 - c) * ROWS, 64)

    def clear(j, _):
        at = (lax.div(j, 16), lax.rem(lax.div(j, 4), 4), lax.rem(j, 4), pl.ds(spare, PAD - ROWS), slice(None))
        weights[at] = jnp.zeros((PAD - ROWS, LANE), BF)
        return 0

    lax.fori_loop(0, 64, clear, 0)

    for lo in range(2):
        load_cot(lo).wait()
        cot_t[lo, :, pl.ds(0, TOK)] = cot[lo, pl.ds(0, TOK), :].T
    for p in range(3):
        ag[p][0].forward()
    for lo in range(2):
        arrive(cot.at[lo, pl.ds(TOK, TOK)], core_send.at[lo], core_recv.at[lo])
        cot_t[lo, :, pl.ds(TOK, TOK)] = cot[lo, pl.ds(TOK, TOK), :].T

    def after(i, step, action):
        pl.when(i == step)(action)

    def each(method, *stages):
        def run():
            for ring in stages:
                getattr(ring, method)()
        return run

    def next_gather(k):
        def run():
            for p in range(3):
                ag[p][k].finish()
                ag[p][k + 1].start()
        return run

    def pass_on(k):
        def run():
            for p in range(3):
                ag[p][k].forward()
        return run

    def term(i, _):
        hi, x = chunk_of(i)
        q = hi * 4 + x
        load_tok(i).wait()
        arrive(tok.at[q, pl.ds(TOK, TOK)], core_send.at[2 + i], core_recv.at[2 + i])
        for lo in range(2):
            part = jnp.dot(
                cot_t[lo, pl.ds(pl.multiple_of(offset, 64), ROWS), :], tok[q],
                preferred_element_type=F32,
            ).astype(BF)
            for y in range(4):
                terms[hi * 2 + lo, x, y] = part[:, y * LANE:(y + 1) * LANE]
        after(i, 0, next_gather(0))
        after(i, 1, pass_on(1))
        after(i, 3, next_gather(1))
        after(i, 3, rs[0][0].start_far)
        after(i, 4, rs[1][0].start_far)
        return 0

    lax.fori_loop(0, N_CHUNK, term, 0)
    rs[2][0].start_far()
    for way in range(2):
        for p in range(3):
            rs[p][0].start_near(way)

    pass_on(2)()
    for p in range(3):
        rs[p][0].combine()
    for p in range(3):
        ag[p][2].finish()

    def next_reduce(k):
        def run():
            for p in range(3):
                rs[p][k].finish()
                rs[p][k + 1].start_far()
                for way in range(2):
                    rs[p][k + 1].start_near(way)
        return run

    def combine(k):
        def run():
            for p in range(3):
                rs[p][k].combine()
        return run

    def update():
        for p in range(3):
            rs[p][2].finish()
        load_state(1).wait()
        load_state(2).wait()
        grad = grad_sum[...] / math.sqrt(TOK * 128)
        one = beta_one * state[1] + (1.0 - beta_one) * grad
        two = beta_two * state[2] + (1.0 - beta_two) * grad * grad
        first_fix = 1.0 - beta_one**step_count
        second_fix = 1.0 - beta_two**step_count
        step = one / first_fix / (jnp.sqrt(two / second_fix) + epsilon)
        moved_master = state[0] - step_size * (step + decay_rate * state[0])
        state_new[0] = moved_master
        state_new[1] = one
        state_new[2] = two
        copy_own[...] = moved_master.astype(BF)
        for k in range(3):
            store_state(k).start()
        store = store_copy()
        store.start()
        for p, (first, count, _) in enumerate(COPY_PARTS):
            push(
                copy_own.at[pl.ds(first, count)],
                copies.at[z_hi, me["x"], me["y"], pl.ds(first, count)],
                nc_send.at[p], nc_recv.at[p], opposite_z,
            )
        store.wait()

    def store_state(k):
        return pltpu.make_async_copy(
            state_new.at[k], (new_master, new_one, new_two)[k], load_sem.at[5 + k]
        )

    def store_copy():
        return pltpu.make_async_copy(
            copy_own, copies.at[z_hi, me["x"], me["y"]], load_sem.at[8]
        )

    def copy_start():
        for p, (first, count, _) in enumerate(COPY_PARTS):
            arrive(
                copies.at[1 - z_hi, me["x"], me["y"], pl.ds(first, count)],
                nc_send.at[p], nc_recv.at[p],
            )
        for p in range(2):
            nc[p][0].start()

    def copy_forward(k):
        def run():
            for p in range(2):
                nc[p][k].forward()
        return run

    def copy_next():
        for p in range(2):
            nc[p][0].finish()
            nc[p][1].start()

    inv_width = 1.0 / math.sqrt(4096)
    inv_hidden = 1.0 / math.sqrt(1792)

    def ig_chunk(i):
        hi, x = chunk_of(i)
        return hi * 4 + x

    def store_ig(i):
        return pltpu.make_async_copy(
            ig_recv.at[i], input_grad.at[:, columns(ig_chunk(i))], ig_out_sem.at[i]
        )

    def close_ig(i):
        arrive(ig_recv.at[i], core_send.at[10 + i], core_recv.at[10 + i])
        total = ig_own[lax.rem(i, 2)] + ig_recv[i].astype(F32)
        ig_recv[i] = (total * inv_hidden).astype(BF)
        store_ig(i).start()

    def against(i, _):
        hi, x = chunk_of(i)
        q = hi * 4 + x
        block = [
            jnp.concatenate([weights[hi * 2 + lo, x, y] for y in range(4)], axis=1)
            for lo in range(2)
        ]

        def backward(first):
            return sum(
                jnp.dot(cot[lo, pl.ds(first, TOK), :], block[lo], preferred_element_type=F32)
                for lo in range(2)
            )

        ig_send[i] = backward(TOK).astype(BF)
        push(ig_send.at[i], ig_recv.at[i], core_send.at[10 + i], core_recv.at[10 + i], sibling)
        ig_own[lax.rem(i, 2)] = backward(0)
        for lo in range(2):
            forward = lax.dot_general(
                tok[q], block[lo], (((1,), (1,)), ((), ())), preferred_element_type=F32
            )

            @pl.when(i == 0)
            def _():
                out_acc[lo] = forward

            @pl.when(i > 0)
            def _():
                out_acc[lo] += forward

        @pl.when(i > 0)
        def _():
            close_ig(i - 1)

        after(i, 1, next_reduce(0))
        after(i, 2, combine(1))
        after(i, 3, next_reduce(1))
        after(i, 4, combine(2))
        after(i, 5, update)
        after(i, 6, copy_start)
        after(i, 7, copy_forward(0))
        return 0

    lax.fori_loop(0, N_CHUNK, against, 0)

    for lo in range(2):
        out_send[lo] = (out_acc[lo, pl.ds(TOK, TOK), :] * inv_width).astype(BF)
        push(out_send.at[lo], out_recv.at[lo], core_send.at[18 + lo], core_recv.at[18 + lo], sibling)
    copy_next()
    close_ig(N_CHUNK - 1)

    for lo in range(2):
        arrive(out_recv.at[lo], core_send.at[18 + lo], core_recv.at[18 + lo])
        own = (out_acc[lo, pl.ds(0, TOK), :] * inv_width).astype(BF)
        theirs = out_recv[lo]

        def write(low, high, lo=lo):
            base = lo * 896
            out_full[:, base:base + 384] = low[:, :384]
            out_full[:, base + 384:base + 512] = low[:, 384:] + high[:, :128]
            out_full[:, base + 512:base + 896] = high[:, 128:]

        @pl.when(c == 0)
        def _():
            write(own, theirs)

        @pl.when(c == 1)
        def _():
            write(theirs, own)

    store_outputs = pltpu.make_async_copy(out_full, outputs, load_sem.at[9])
    store_outputs.start()
    copy_forward(1)()
    for p in range(2):
        nc[p][1].finish()

    for k in range(3):
        store_state(k).wait()
    store_outputs.wait()
    for i in range(N_CHUNK):
        store_ig(i).wait()

    for p in range(3):
        for k in range(3):
            ag[p][k].close()
            rs[p][k].close()
    for p, (first, count, _) in enumerate(COPY_PARTS):
        left(copy_own.at[pl.ds(first, count)], nc_send.at[p], nc_recv.at[p])
        for k in range(2):
            nc[p][k].close()
    for lo in range(2):
        left(cot.at[lo, pl.ds(TOK, TOK)], core_send.at[lo], core_recv.at[lo])
        left(out_send.at[lo], core_send.at[18 + lo], core_recv.at[18 + lo])
    for i in range(N_CHUNK):
        left(tok.at[0, pl.ds(TOK, TOK)], core_send.at[2 + i], core_recv.at[2 + i])
        left(ig_send.at[i], core_send.at[10 + i], core_recv.at[10 + i])


def local(tokens, cotangent, master, moment_one, moment_two):
    vmem = pltpu.VMEM
    dma = pltpu.SemaphoreType.DMA
    hidden = cotangent.shape[1]
    width = tokens.shape[1]
    anywhere = pl.BlockSpec(memory_space=pl.ANY)
    state_shape = jax.ShapeDtypeStruct((ROWS, LANE), F32)
    got = []
    for stage in range(3):
        for p, (_, count, order) in enumerate(PARTS):
            if stage == 0:
                last = order[0]
                dims = tuple(2 if n == last else 4 for n in AXES if n != order[2])
                got.append(vmem((6,) + dims + (count, LANE), BF))
            elif stage == 1:
                got.append(vmem((6, 2, count, LANE), BF))
            else:
                got.append(vmem((6, count // 2, LANE), BF))
    results = pl.pallas_call(
        kernel,
        out_shape=(
            jax.ShapeDtypeStruct((TOK, hidden), BF),
            jax.ShapeDtypeStruct((TOK, width), BF),
            state_shape, state_shape, state_shape,
            jax.ShapeDtypeStruct((2, 4, 4, ROWS, LANE), BF),
        ),
        in_specs=[anywhere] * 5,
        out_specs=(anywhere,) * 6,
        scratch_shapes=[
            vmem((N_CHUNK, 2 * TOK, CHUNK), BF),
            vmem((2, 2 * TOK, PAD), BF),
            vmem((2, PAD, 2 * TOK), BF),
            vmem((4, 4, 4, PAD, LANE), BF),
            vmem((4, 4, 4, ROWS, LANE), BF),
            *got,
            vmem((ROWS, LANE), F32),
            vmem((2, 2 * TOK, PAD), F32),
            vmem((2, TOK, CHUNK), F32),
            vmem((N_CHUNK, TOK, CHUNK), BF),
            vmem((N_CHUNK, TOK, CHUNK), BF),
            vmem((2, TOK, PAD), BF),
            vmem((2, TOK, PAD), BF),
            vmem((TOK, hidden), BF),
            vmem((3, ROWS, LANE), F32),
            vmem((3, ROWS, LANE), F32),
            vmem((ROWS, LANE), BF),
            dma((10,)), dma((N_CHUNK,)), dma((N_CHUNK,)),
            dma((20,)), dma((20,)), dma((54,)), dma((54,)), dma((54,)), dma((54,)),
            dma((26,)), dma((26,)),
        ],
        compiler_params=pltpu.CompilerParams(
            collective_id=0, has_side_effects=True, vmem_limit_bytes=63 * 2**20
        ),
        name="step",
    )(tokens, cotangent, master, moment_one, moment_two)
    *rest, copies = results
    new_copy = copies.transpose(3, 0, 1, 2, 4).reshape(ROWS, width)
    return (*rest, new_copy)


def solution(mesh):
    placed = (
        P(("node", "dp"), None),
        P(("node", "dp"), None),
        P("node", "dp"),
        P("node", "dp"),
        P("node", "dp"),
    )
    return jax.shard_map(
        local,
        mesh=mesh,
        in_specs=placed,
        out_specs=(
            P(("node", "dp"), None),
            P(("node", "dp"), None),
            P("node", "dp"),
            P("node", "dp"),
            P("node", "dp"),
            P("node", None),
        ),
        check_vma=False,
    )
```

```python
import math

import jax
import jax.numpy as jnp
from jax import lax
from jax.experimental import pallas as pl
from jax.experimental.pallas import tpu as pltpu
from jax.sharding import PartitionSpec as P

beta_one = 0.9
beta_two = 0.95
epsilon = 1e-08
step_size = 0.2
decay_rate = 0.1
step_count = 10

MESH = pl.DeviceIdType.MESH
AXES = ("z", "x", "y")
BF = jnp.bfloat16
F32 = jnp.float32

ROWS = 448
PAD = 512
LANE = 128
TOK = 512
CHUNK = 512
N_CHUNK = 8
REDUCE_PARTS = ((0, 160, "zxy"), (160, 144, "xyz"), (304, 144, "yzx"))
GATHER_PARTS = (
    (0, 256, "z", "x", "y", ((0, 96, "y", "x"), (96, 160, "x", "y"))),
    (256, 96, "x", "z", "y", ((256, 96, "y", "z"),)),
    (352, 96, "y", "x", "z", ((352, 96, "z", "x"),)),
)
COPY_PARTS = ((0, 224, "xy"), (224, 224, "yx"))
REDUCE_TURNS = (2, 1, 3, 0)
GATHER_TURNS = (0, 1, 3, 2)
FAR = (1, 3, 2)


def device_at(co):
    return (
        lax.rem(co["z"], 2) * 2 + co["c"],
        lax.div(co["z"], 2) * 16 + co["x"] * 4 + co["y"],
    )


def moved(co, axis, by):
    other = dict(co)
    other[axis] = lax.rem(co[axis] + by + 4, 4)
    return other


def kernel(
    tokens, cotangent, master, moment_one, moment_two,
    out_full, ig_recv, state_new, copies,
    tok, cot, cot_t, weights, terms,
    got1a, got1b, got1c, got2a, got2b, got2c, got3a, got3b, got3c,
    grad_sum, out_acc, ig_own, ig_send, out_send, out_recv, state,
    load_sem, tok_sem,
    core_send, core_recv, ag_send, ag_recv, rs_send, rs_recv, nc_send, nc_recv,
):
    node = lax.axis_index("node")
    dp = lax.axis_index("dp")
    c = lax.rem(node, 2)
    z_lo = lax.div(node, 2)
    z_hi = lax.div(dp, 16)
    me = {
        "z": z_hi * 2 + z_lo,
        "x": lax.rem(lax.div(dp, 4), 4),
        "y": lax.rem(dp, 4),
        "c": c,
    }
    sibling = device_at({**me, "c": 1 - c})
    opposite_z = device_at(moved(me, "z", 2))
    window = [pl.multiple_of(lo * 896 + c * 384, 128) for lo in range(2)]
    sib_window = [pl.multiple_of(lo * 896 + (1 - c) * 384, 128) for lo in range(2)]
    offset = c * 64

    def remote(src, dst, send, recv, to):
        return pltpu.make_async_remote_copy(
            src_ref=src, dst_ref=dst, send_sem=send, recv_sem=recv,
            device_id=to, device_id_type=MESH,
        )

    def push(src, dst, send, recv, to):
        remote(src, dst, send, recv, to).start()

    def left(src, send, recv):
        remote(src, src, send, recv, sibling).wait_send()

    def arrive(dst, send, recv):
        remote(dst, dst, send, recv, sibling).wait_recv()

    def load_state(k):
        return pltpu.make_async_copy(
            (master, moment_one, moment_two)[k], state.at[k], load_sem.at[k]
        )

    def load_cot(lo):
        return pltpu.make_async_copy(
            cotangent.at[:, pl.ds(window[lo], PAD)],
            cot.at[lo, pl.ds(0, TOK)],
            load_sem.at[3 + lo],
        )

    def half_of(i):
        return lax.rem(z_hi + 1 + i, 2)

    def term_chunk(i):
        j = lax.div(i, 2)
        turn = 2 - j + lax.div(j, 2) * (3 - 2 * lax.rem(j, 2))
        return half_of(i), lax.rem(me["x"] + turn + 4, 4)

    def pass_chunk(i):
        j = lax.div(i, 2)
        turn = j + lax.div(j, 2) * (1 - 2 * lax.rem(j, 2))
        return half_of(i), lax.rem(me["x"] + turn, 4)

    def columns(q):
        return pl.ds(pl.multiple_of(q * CHUNK, CHUNK), CHUNK)

    def load_tok(i):
        hi, x = term_chunk(i)
        q = hi * 4 + x
        return pltpu.make_async_copy(
            tokens.at[:, columns(q)], tok.at[q, pl.ds(0, TOK)], tok_sem.at[i]
        )

    barrier = pltpu.get_barrier_semaphore()
    peers = [sibling]
    for axis in AXES:
        peers += [device_at(moved(me, axis, by)) for by in FAR]
    for peer in peers:
        pl.semaphore_signal(barrier, inc=1, device_id=peer, device_id_type=MESH)
    load_state(0).start()
    load_cot(0).start()
    load_cot(1).start()
    for i in range(N_CHUNK):
        load_tok(i).start()
    load_state(1).start()
    load_state(2).start()

    spare = pl.multiple_of((1 - c) * ROWS, 64)

    def clear(j, _):
        at = (lax.div(j, 16), lax.rem(lax.div(j, 4), 4), lax.rem(j, 4), pl.ds(spare, PAD - ROWS), slice(None))
        weights[at] = jnp.zeros((PAD - ROWS, LANE), BF)
        return 0

    lax.fori_loop(0, 64, clear, 0)
    pl.semaphore_wait(barrier, len(peers))

    def place(axis, by):
        return lax.rem(me[axis] + by + 4, 4)

    def pair(half):
        return pl.ds(2 * half, 2)

    every = slice(None)

    class Gather:
        def __init__(self, first, count, ring, turn_axis, half_axis, planes, base):
            self.first, self.count, self.ring = first, count, ring
            self.turn_axis, self.half_axis, self.planes = turn_axis, half_axis, planes
            self.base = base

        def at(self, spec, first, count):
            rows = pl.ds(pl.multiple_of(offset + first, 16), count)
            spec = {**{axis: me[axis] for axis in AXES}, **spec}
            return weights.at[spec["z"], spec["x"], spec["y"], rows, :]

        def sems(self, k):
            return ag_send.at[self.base + k], ag_recv.at[self.base + k]

        def first_start(self):
            for n, (first, count, one, two) in enumerate(self.planes):
                for by in FAR:
                    ref = self.at({}, first, count)
                    push(ref, ref, *self.sems(n * 6 + by - 1), device_at(moved(me, one, by)))

        def first_wait(self):
            for n, (first, count, one, two) in enumerate(self.planes):
                for by in FAR:
                    arrive(self.at({one: place(one, -by)}, first, count), *self.sems(n * 6 + by - 1))

        def second_start(self):
            for n, (first, count, one, two) in enumerate(self.planes):
                for by in FAR:
                    ref = self.at({one: every}, first, count)
                    push(ref, ref, *self.sems(n * 6 + 2 + by), device_at(moved(me, two, by)))

        def second_wait(self):
            for n, (first, count, one, two) in enumerate(self.planes):
                for by in FAR:
                    arrive(self.at({one: every, two: place(two, -by)}, first, count), *self.sems(n * 6 + 2 + by))

        def part(self, turn, half, where):
            spec = {
                self.turn_axis: place(self.turn_axis, GATHER_TURNS[turn]),
                self.half_axis: pair(half),
                self.ring: place(self.ring, where),
            }
            return self.at(spec, self.first, self.count)

        def ring_sems(self, turn, way, message):
            return self.sems(12 + turn * 6 + way * 3 + message)

        def start(self, turn):
            for message in range(2):
                for way in range(2):
                    ref = self.part(turn, message if way == 0 else 1 - message, 0)
                    push(ref, ref, *self.ring_sems(turn, way, message), device_at(moved(me, self.ring, 1 - 2 * way)))

        def forward(self, turn):
            for way in range(2):
                ref = self.part(turn, way, 2 * way - 1)
                arrive(ref, *self.ring_sems(turn, way, 0))
                push(ref, ref, *self.ring_sems(turn, way, 2), device_at(moved(me, self.ring, 1 - 2 * way)))

        def finish(self, turn):
            for way in range(2):
                arrive(self.part(turn, 1 - way, 2 * way - 1), *self.ring_sems(turn, way, 1))
                arrive(self.part(turn, way, 2), *self.ring_sems(turn, way, 2))

        def close(self):
            for n, (first, count, one, two) in enumerate(self.planes):
                for by in FAR:
                    left(self.at({}, first, count), *self.sems(n * 6 + by - 1))
                    left(self.at({one: every}, first, count), *self.sems(n * 6 + 2 + by))
            for turn in range(4):
                for k in range(6):
                    left(self.part(turn, 0, 0), *self.sems(12 + turn * 6 + k))

    ag = [Gather(*part, p * 36) for p, part in enumerate(GATHER_PARTS)]
    ag_z, ag_x, ag_y = ag

    class Copies:
        def __init__(self, order, first, count, z_half, base):
            self.one, self.two = order
            self.first, self.count, self.z_half, self.base = first, count, z_half, base

        def at(self, one, two, half=None):
            spec = {self.one: one, self.two: two}
            rows = pl.ds(self.first, self.count)
            if half is not None:
                rows = pl.ds(self.first + half * self.count // 2, self.count // 2)
            return copies.at[self.z_half, spec["x"], spec["y"], rows, :]

        def sems(self, k):
            return nc_send.at[self.base + k], nc_recv.at[self.base + k]

        def first_start(self):
            ref = self.at(me[self.one], me[self.two])
            for by in FAR:
                push(ref, ref, *self.sems(by - 1), device_at(moved(me, self.one, by)))

        def first_wait(self, by):
            arrive(self.at(place(self.one, -by), me[self.two]), *self.sems(by - 1))

        def part(self, by, half, where):
            return self.at(place(self.one, by), place(self.two, where), half)

        def ring_sems(self, by, way, message):
            return self.sems(3 + by * 6 + way * 3 + message)

        def start(self, by):
            for message in range(2):
                for way in range(2):
                    ref = self.part(by, message if way == 0 else 1 - message, 0)
                    push(ref, ref, *self.ring_sems(by, way, message), device_at(moved(me, self.two, 1 - 2 * way)))

        def forward(self, by):
            for way in range(2):
                ref = self.part(by, way, 2 * way - 1)
                arrive(ref, *self.ring_sems(by, way, 0))
                push(ref, ref, *self.ring_sems(by, way, 2), device_at(moved(me, self.two, 1 - 2 * way)))

        def finish(self, by):
            for way in range(2):
                arrive(self.part(by, 1 - way, 2 * way - 1), *self.ring_sems(by, way, 1))
                arrive(self.part(by, way, 2), *self.ring_sems(by, way, 2))

        def close(self):
            for by in FAR:
                left(self.at(me[self.one], me[self.two]), *self.sems(by - 1))
            for by in range(4):
                for k in range(6):
                    left(self.part(by, 0, 0), *self.sems(3 + by * 6 + k))

    nc = [
        [
            Copies(order, first, count, z_half, 2 + (g * 2 + p) * 27)
            for p, (first, count, order) in enumerate(COPY_PARTS)
        ]
        for g, z_half in enumerate((z_hi, 1 - z_hi))
    ]

    class Reduce:
        def __init__(self, order, first, count, got, base):
            self.one, self.two, self.three = order
            self.rows = pl.ds(first, count)
            self.got1, self.got2, self.got3 = got
            self.base = base

        def index(self, one, two, three):
            spec = {self.one: one, self.two: two, self.three: three}
            return spec["z"], spec["x"], spec["y"], self.rows, every

        def sems(self, k):
            return rs_send.at[self.base + k], rs_recv.at[self.base + k]

        def ring_index(self, turn, where, half):
            return self.index(place(self.one, where), place(self.two, REDUCE_TURNS[turn]), pair(half))

        def out(self, turn, where, half, slot, way):
            push(
                terms.at[self.ring_index(turn, where, half)], self.got1.at[turn, slot],
                *self.sems(turn * 6 + slot), device_at(moved(me, self.one, 1 - 2 * way)),
            )

        def far(self, turn):
            self.out(turn, 2, 0, 0, 0)
            self.out(turn, 2, 1, 1, 1)

        def near(self, turn, way):
            if way == 0:
                self.out(turn, 1, 1, 3, 0)
            else:
                self.out(turn, -1, 0, 5, 1)

        def combine(self, turn):
            for way in range(2):
                arrive(self.got1.at[turn, way], *self.sems(turn * 6 + way))
                at = self.ring_index(turn, 1 - 2 * way, way)
                total = terms[at].astype(F32) + self.got1[turn, way].astype(F32)
                terms[at] = total.astype(BF)
                self.out(turn, 1 - 2 * way, way, 2 if way == 0 else 4, way)

        def line(self, by):
            return self.index(me[self.one], place(self.two, by), every)

        def finish(self, turn):
            for half, (one, two) in enumerate(((2, 5), (3, 4))):
                arrive(self.got1.at[turn, one], *self.sems(turn * 6 + one))
                arrive(self.got1.at[turn, two], *self.sems(turn * 6 + two))
                at = self.ring_index(turn, 0, half)
                total = (
                    terms[at].astype(F32)
                    + self.got1[turn, one].astype(F32)
                    + self.got1[turn, two].astype(F32)
                )
                terms[at] = total.astype(BF)
            by = REDUCE_TURNS[turn]
            if by:
                push(
                    terms.at[self.line(by)], self.got2.at[by - 1],
                    *self.sems(23 + by), device_at(moved(me, self.two, by)),
                )

        def second(self):
            for by in FAR:
                arrive(self.got2.at[by - 1], *self.sems(23 + by))
            total = terms[self.line(0)].astype(F32)
            for k in range(3):
                total += self.got2[k].astype(F32)
            terms[self.line(0)] = total.astype(BF)
            for by in FAR:
                push(
                    terms.at[self.index(me[self.one], me[self.two], place(self.three, by))],
                    self.got3.at[by - 1], *self.sems(26 + by), device_at(moved(me, self.three, by)),
                )

        def third(self):
            for by in FAR:
                arrive(self.got3.at[by - 1], *self.sems(26 + by))
            total = terms[self.index(me[self.one], me[self.two], me[self.three])].astype(F32)
            for k in range(3):
                total += self.got3[k].astype(F32)
            grad_sum[self.rows, :] = total

        def close(self):
            for turn in range(4):
                for slot in range(6):
                    left(self.got1.at[turn, slot], *self.sems(turn * 6 + slot))
            for by in FAR:
                left(self.got2.at[by - 1], *self.sems(23 + by))
                left(self.got3.at[by - 1], *self.sems(26 + by))

    got = ((got1a, got2a, got3a), (got1b, got2b, got3b), (got1c, got2c, got3c))
    rs = [
        Reduce(order, first, count, got[p], p * 30)
        for p, (first, count, order) in enumerate(REDUCE_PARTS)
    ]
    rs_z, rs_x, rs_y = rs

    for lo in range(2):
        push(
            cotangent.at[:, pl.ds(sib_window[lo], PAD)], cot.at[lo, pl.ds(TOK, TOK)],
            core_send.at[lo], core_recv.at[lo], sibling,
        )
    for i in range(N_CHUNK):
        hi, x = term_chunk(i)
        q = hi * 4 + x
        push(
            tokens.at[:, columns(q)], tok.at[q, pl.ds(TOK, TOK)],
            core_send.at[2 + i], core_recv.at[2 + i], sibling,
        )

    load_state(0).wait()
    weights[me["z"], me["x"], me["y"], pl.ds(pl.multiple_of(offset, 32), ROWS), :] = state[0].astype(BF)
    for part in ag:
        part.first_start()
    for lo in range(2):
        load_cot(lo).wait()
        cot_t[lo, :, pl.ds(0, TOK)] = cot[lo, pl.ds(0, TOK), :].T
    for lo in range(2):
        arrive(cot.at[lo, pl.ds(TOK, TOK)], core_send.at[lo], core_recv.at[lo])
        cot_t[lo, :, pl.ds(TOK, TOK)] = cot[lo, pl.ds(TOK, TOK), :].T

    for part in ag:
        part.first_wait()
        part.second_start()

    def send_turn(parts, turn):
        for part in parts:
            part.far(turn)
            for way in range(2):
                part.near(turn, way)

    def term(i, _):
        hi, x = term_chunk(i)
        q = hi * 4 + x
        load_tok(i).wait()
        arrive(tok.at[q, pl.ds(TOK, TOK)], core_send.at[2 + i], core_recv.at[2 + i])
        for lo in range(2):
            part = jnp.dot(
                cot_t[lo, pl.ds(pl.multiple_of(offset, 64), ROWS), :], tok[q],
                preferred_element_type=F32,
            ).astype(BF)
            for y in range(4):
                terms[hi * 2 + lo, x, y] = part[:, y * LANE:(y + 1) * LANE]

        @pl.when(i == 1)
        def _():
            send_turn((rs_z,), 0)
            for turn in range(2):
                rs_x.far(turn)

        @pl.when(i == 3)
        def _():
            send_turn((rs_z,), 1)
            for turn in range(2):
                rs_x.near(turn, 0)

        @pl.when(i == 5)
        def _():
            for turn in range(2):
                rs_x.near(turn, 1)

        return 0

    lax.fori_loop(0, N_CHUNK, term, 0)

    def gather(action, *args):
        for part in ag:
            getattr(part, action)(*args)

    def reduce(action, *args):
        for part in rs:
            getattr(part, action)(*args)

    first = (rs_z, rs_x)

    def both(action, turn):
        for part in first:
            getattr(part, action)(turn)

    send_turn((rs_y,), 0)
    send_turn((rs_y,), 1)
    both("combine", 0)
    send_turn(first, 2)
    both("combine", 1)
    rs_y.combine(0)
    reduce("finish", 0)
    send_turn(rs, 3)
    send_turn((rs_y,), 2)
    rs_y.combine(1)
    both("combine", 2)
    reduce("finish", 1)
    gather("second_wait")
    rs_y.combine(2)
    both("combine", 3)
    reduce("finish", 2)
    rs_y.combine(3)
    gather("start", 0)
    ag_x.start(1)
    reduce("finish", 3)
    gather("forward", 0)
    ag_x.forward(1)
    reduce("second")
    ag_z.start(1)
    ag_x.start(2)
    ag_x.start(3)
    reduce("third")

    def update():
        load_state(1).wait()
        load_state(2).wait()
        grad = grad_sum[...] / math.sqrt(TOK * 128)
        one = beta_one * state[1] + (1.0 - beta_one) * grad
        two = beta_two * state[2] + (1.0 - beta_two) * grad * grad
        first_fix = 1.0 - beta_one**step_count
        second_fix = 1.0 - beta_two**step_count
        step = one / first_fix / (jnp.sqrt(two / second_fix) + epsilon)
        moved_master = state[0] - step_size * (step + decay_rate * state[0])
        state_new[0] = moved_master
        state_new[1] = one
        state_new[2] = two
        copies[z_hi, me["x"], me["y"]] = moved_master.astype(BF)
        for p, (first, count, _) in enumerate(COPY_PARTS):
            ref = copies.at[z_hi, me["x"], me["y"], pl.ds(first, count)]
            push(ref, ref, nc_send.at[p], nc_recv.at[p], opposite_z)
        for part in nc[0]:
            part.first_start()
            part.start(0)

    def copies_rest(g):
        def run():
            for by in FAR:
                for part in nc[g]:
                    part.first_wait(by)
                    part.start(4 - by)
        return run

    def copies_other():
        for p, (first, count, _) in enumerate(COPY_PARTS):
            arrive(
                copies.at[1 - z_hi, me["x"], me["y"], pl.ds(first, count)],
                nc_send.at[p], nc_recv.at[p],
            )
        for part in nc[1]:
            part.first_start()
            part.start(0)

    def copies_forward(g, *turns):
        def run():
            for by in turns:
                for part in nc[g]:
                    part.forward(by)
        return run

    def after_pass(step):
        if step == 0:
            copies_rest(0)()
            ag_x.forward(2)
            ag_x.forward(3)
            ag_z.forward(1)
            ag_y.forward(1)
        if step == 1:
            copies_other()
            ag_z.start(2)
            ag_y.start(2)
        if step == 2:
            copies_rest(1)()
            copies_forward(0, 0)()
            for turn in (1, 2, 3):
                ag_x.finish(turn)
            ag_z.finish(1)
            ag_y.finish(1)
        if step == 3:
            copies_forward(0, 3)()
            ag_z.forward(2)
            ag_y.forward(2)
        if step == 4:
            copies_forward(0, 1)()
            copies_forward(1, 0)()
            ag_z.start(3)
            ag_y.start(3)
        if step == 5:
            copies_forward(0, 2)()
            ag_z.finish(2)
            ag_y.finish(2)
        if step == 6:
            ag_z.forward(3)
            ag_y.forward(3)
            copies_forward(1, 3)()
        if step == 7:
            copies_forward(1, 1)()
        if step == 8:
            copies_forward(1, 2)()
            ag_z.finish(3)
            ag_y.finish(3)

    update()
    ag_y.start(1)
    gather("finish", 0)

    inv_width = 1.0 / math.sqrt(4096)
    inv_hidden = 1.0 / math.sqrt(1792)

    def ig_chunk(i):
        hi, x = pass_chunk(i)
        return hi * 4 + x

    def close_ig(i):
        q = ig_chunk(i)
        arrive(ig_recv.at[q], core_send.at[10 + i], core_recv.at[10 + i])
        total = ig_own[lax.rem(i, 2)] + ig_recv[q].astype(F32)
        ig_recv[q] = (total * inv_hidden).astype(BF)

    def against(j, _):
        chunks = [pass_chunk(2 * j + k) for k in range(2)]
        block = [
            [
                jnp.concatenate([weights[hi * 2 + lo, x, y] for y in range(4)], axis=1)
                for lo in range(2)
            ]
            for hi, x in chunks
        ]

        def events(k):
            for pair_at in range(4):
                if 3 * pair_at + k < 9:
                    pl.when(j == pair_at)(lambda step=3 * pair_at + k: after_pass(step))

        for k, (hi, x) in enumerate(chunks):
            q = hi * 4 + x
            i = 2 * j + k

            def backward(first):
                return sum(
                    jnp.dot(cot[lo, pl.ds(first, TOK), :], block[k][lo], preferred_element_type=F32)
                    for lo in range(2)
                )

            ig_send[i] = backward(TOK).astype(BF)
            push(ig_send.at[i], ig_recv.at[q], core_send.at[10 + i], core_recv.at[10 + i], sibling)
            ig_own[k] = backward(0)
            if k:
                close_ig(i - 1)
            else:

                @pl.when(j > 0)
                def _():
                    close_ig(i - 1)

            events(k)

        both = jnp.concatenate([tok[hi * 4 + x] for hi, x in chunks], axis=1)
        for lo in range(2):
            forward = lax.dot_general(
                both, jnp.concatenate([block[k][lo] for k in range(2)], axis=1),
                (((1,), (1,)), ((), ())), preferred_element_type=F32,
            )

            @pl.when(j == 0)
            def _():
                out_acc[lo] = forward

            @pl.when(j > 0)
            def _():
                out_acc[lo] += forward

        events(2)
        return 0

    lax.fori_loop(0, N_CHUNK // 2, against, 0)

    for lo in range(2):
        out_send[lo] = (out_acc[lo, pl.ds(TOK, TOK), :] * inv_width).astype(BF)
        push(out_send.at[lo], out_recv.at[lo], core_send.at[18 + lo], core_recv.at[18 + lo], sibling)
    close_ig(N_CHUNK - 1)

    for lo in range(2):
        arrive(out_recv.at[lo], core_send.at[18 + lo], core_recv.at[18 + lo])
        own = (out_acc[lo, pl.ds(0, TOK), :] * inv_width).astype(BF)
        theirs = out_recv[lo]

        def write(low, high, lo=lo):
            base = lo * 896
            out_full[:, base:base + 384] = low[:, :384]
            out_full[:, base + 384:base + 512] = low[:, 384:] + high[:, :128]
            out_full[:, base + 512:base + 896] = high[:, 128:]

        @pl.when(c == 0)
        def _():
            write(own, theirs)

        @pl.when(c == 1)
        def _():
            write(theirs, own)

    for g in range(2):
        for by in range(4):
            for part in nc[g]:
                part.finish(by)

    gather("close")
    reduce("close")
    for p, (first, count, _) in enumerate(COPY_PARTS):
        left(
            copies.at[z_hi, me["x"], me["y"], pl.ds(first, count)], nc_send.at[p], nc_recv.at[p]
        )
        for g in range(2):
            nc[g][p].close()
    for lo in range(2):
        left(cot.at[lo, pl.ds(TOK, TOK)], core_send.at[lo], core_recv.at[lo])
        left(out_send.at[lo], core_send.at[18 + lo], core_recv.at[18 + lo])
    for i in range(N_CHUNK):
        left(tok.at[0, pl.ds(TOK, TOK)], core_send.at[2 + i], core_recv.at[2 + i])
        left(ig_send.at[i], core_send.at[10 + i], core_recv.at[10 + i])


def local(tokens, cotangent, master, moment_one, moment_two):
    vmem = pltpu.VMEM
    dma = pltpu.SemaphoreType.DMA
    hidden = cotangent.shape[1]
    width = tokens.shape[1]
    anywhere = pl.BlockSpec(memory_space=pl.ANY)
    state_shape = jax.ShapeDtypeStruct((ROWS, LANE), F32)
    got = []
    for _, count, _ in REDUCE_PARTS:
        got.append(vmem((4, 6, 2, count, LANE), BF))
    for _, count, _ in REDUCE_PARTS:
        got.append(vmem((3, 4, count, LANE), BF))
    for _, count, _ in REDUCE_PARTS:
        got.append(vmem((3, count, LANE), BF))
    inside = pl.BlockSpec(memory_space=vmem)
    held = pl.pallas_call(
        kernel,
        out_shape=(
            vmem((TOK, hidden), BF),
            vmem((N_CHUNK, TOK, CHUNK), BF),
            vmem((3, ROWS, LANE), F32),
            vmem((2, 4, 4, ROWS, LANE), BF),
        ),
        in_specs=[anywhere] * 5,
        out_specs=(inside,) * 4,
        scratch_shapes=[
            vmem((N_CHUNK, 2 * TOK, CHUNK), BF),
            vmem((2, 2 * TOK, PAD), BF),
            vmem((2, PAD, 2 * TOK), BF),
            vmem((4, 4, 4, PAD, LANE), BF),
            vmem((4, 4, 4, ROWS, LANE), BF),
            *got,
            vmem((ROWS, LANE), F32),
            vmem((2, 2 * TOK, PAD), F32),
            vmem((2, TOK, CHUNK), F32),
            vmem((N_CHUNK, TOK, CHUNK), BF),
            vmem((2, TOK, PAD), BF),
            vmem((2, TOK, PAD), BF),
            vmem((3, ROWS, LANE), F32),
            dma((5,)), dma((N_CHUNK,)),
            dma((20,)), dma((20,)), dma((108,)), dma((108,)), dma((90,)), dma((90,)),
            dma((110,)), dma((110,)),
        ],
        compiler_params=pltpu.CompilerParams(
            collective_id=0, has_side_effects=True, vmem_limit_bytes=54 * 2**20
        ),
        name="step",
    )(tokens, cotangent, master, moment_one, moment_two)
    return pl.pallas_call(
        store,
        out_shape=(
            jax.ShapeDtypeStruct((TOK, hidden), BF),
            jax.ShapeDtypeStruct((TOK, width), BF),
            state_shape, state_shape, state_shape,
            jax.ShapeDtypeStruct((ROWS, width), BF),
        ),
        in_specs=[anywhere] * 4,
        out_specs=(anywhere,) * 6,
        scratch_shapes=[dma((44,))],
        compiler_params=pltpu.CompilerParams(has_side_effects=True, vmem_limit_bytes=2**20),
        name="store",
    )(*held)


def store(
    out_full, ig_full, state_new, copies,
    outputs, input_grad, new_master, new_one, new_two, new_copy, sem,
):
    moves = [(out_full, outputs)]
    for q in range(N_CHUNK):
        moves.append((ig_full.at[q], input_grad.at[:, pl.ds(q * CHUNK, CHUNK)]))
    for k, ref in enumerate((new_master, new_one, new_two)):
        moves.append((state_new.at[k], ref))
    for b in range(32):
        moves.append((
            copies.at[b // 16, (b // 4) % 4, b % 4], new_copy.at[:, pl.ds(b * LANE, LANE)],
        ))
    pending = [pltpu.make_async_copy(src, dst, sem.at[k]) for k, (src, dst) in enumerate(moves)]
    for copy in pending:
        copy.start()
    for copy in pending:
        copy.wait()


def solution(mesh):
    placed = (
        P(("node", "dp"), None),
        P(("node", "dp"), None),
        P("node", "dp"),
        P("node", "dp"),
        P("node", "dp"),
    )
    return jax.shard_map(
        local,
        mesh=mesh,
        in_specs=placed,
        out_specs=(
            P(("node", "dp"), None),
            P(("node", "dp"), None),
            P("node", "dp"),
            P("node", "dp"),
            P("node", "dp"),
            P("node", None),
        ),
        check_vma=False,
    )
```

```python
import math

import jax
import jax.numpy as jnp
from jax import lax
from jax.experimental import pallas as pl
from jax.experimental.pallas import tpu as pltpu
from jax.sharding import PartitionSpec as P

beta_one = 0.9
beta_two = 0.95
epsilon = 1e-08
step_size = 0.2
decay_rate = 0.1
step_count = 10

MESH = pl.DeviceIdType.MESH
AXES = ("z", "x", "y")
BF = jnp.bfloat16
F32 = jnp.float32

ROWS = 448
PAD = 512
LANE = 128
TOK = 512
CHUNK = 512
N_CHUNK = 8
REDUCE_PARTS = ((0, 160, "zxy"), (160, 144, "xyz"), (304, 144, "yzx"))
GATHER_PARTS = (
    (0, 256, "z", "x", "y", ((0, 96, "y", "x"), (96, 160, "x", "y"))),
    (256, 96, "x", "z", "y", ((256, 96, "y", "z"),)),
    (352, 96, "y", "x", "z", ((352, 96, "z", "x"),)),
)
COPY_PARTS = ((0, 224, "xy"), (224, 224, "yx"))
REDUCE_TURNS = (2, 1, 3, 0)
GATHER_TURNS = (0, 1, 3, 2)
FAR = (1, 3, 2)


def device_at(co):
    return (
        lax.rem(co["z"], 2) * 2 + co["c"],
        lax.div(co["z"], 2) * 16 + co["x"] * 4 + co["y"],
    )


def moved(co, axis, by):
    other = dict(co)
    other[axis] = lax.rem(co[axis] + by + 4, 4)
    return other


def kernel(
    tokens, cotangent, master, moment_one, moment_two,
    out_full, ig_recv, state_new, copies,
    tok, cot, cot_t, weights, terms,
    got1a, got1b, got1c, got2a, got2b, got2c, got3a, got3b, got3c,
    grad_sum, out_acc, ig_own, ig_send, out_send, out_recv, state,
    load_sem, tok_sem,
    core_send, core_recv, ag_send, ag_recv, rs_send, rs_recv, nc_send, nc_recv,
):
    node = lax.axis_index("node")
    dp = lax.axis_index("dp")
    c = lax.rem(node, 2)
    z_lo = lax.div(node, 2)
    z_hi = lax.div(dp, 16)
    me = {
        "z": z_hi * 2 + z_lo,
        "x": lax.rem(lax.div(dp, 4), 4),
        "y": lax.rem(dp, 4),
        "c": c,
    }
    sibling = device_at({**me, "c": 1 - c})
    opposite_z = device_at(moved(me, "z", 2))
    window = [pl.multiple_of(lo * 896 + c * 384, 128) for lo in range(2)]
    sib_window = [pl.multiple_of(lo * 896 + (1 - c) * 384, 128) for lo in range(2)]
    offset = c * 64

    def remote(src, dst, send, recv, to):
        return pltpu.make_async_remote_copy(
            src_ref=src, dst_ref=dst, send_sem=send, recv_sem=recv,
            device_id=to, device_id_type=MESH,
        )

    def push(src, dst, send, recv, to):
        remote(src, dst, send, recv, to).start()

    def left(src, send, recv):
        remote(src, src, send, recv, sibling).wait_send()

    def arrive(dst, send, recv):
        remote(dst, dst, send, recv, sibling).wait_recv()

    def load_state(k):
        return pltpu.make_async_copy(
            (master, moment_one, moment_two)[k], state.at[k], load_sem.at[k]
        )

    def load_cot(lo):
        return pltpu.make_async_copy(
            cotangent.at[:, pl.ds(window[lo], PAD)],
            cot.at[lo, pl.ds(0, TOK)],
            load_sem.at[3 + lo],
        )

    def half_of(i):
        return lax.rem(z_hi + 1 + i, 2)

    def term_chunk(i):
        j = lax.div(i, 2)
        turn = 2 - j + lax.div(j, 2) * (3 - 2 * lax.rem(j, 2))
        return half_of(i), lax.rem(me["x"] + turn + 4, 4)

    def pass_chunk(i):
        j = lax.div(i, 2)
        turn = j + lax.div(j, 2) * (1 - 2 * lax.rem(j, 2))
        return half_of(i), lax.rem(me["x"] + turn, 4)

    def columns(q):
        return pl.ds(pl.multiple_of(q * CHUNK, CHUNK), CHUNK)

    def load_tok(i):
        hi, x = term_chunk(i)
        q = hi * 4 + x
        return pltpu.make_async_copy(
            tokens.at[:, columns(q)], tok.at[q, pl.ds(0, TOK)], tok_sem.at[i]
        )

    barrier = pltpu.get_barrier_semaphore()
    peers = [sibling]
    for axis in AXES:
        peers += [device_at(moved(me, axis, by)) for by in FAR]
    for peer in peers:
        pl.semaphore_signal(barrier, inc=1, device_id=peer, device_id_type=MESH)
    load_state(0).start()
    load_cot(0).start()
    load_cot(1).start()
    for i in range(N_CHUNK):
        load_tok(i).start()
    load_state(1).start()
    load_state(2).start()

    spare = pl.multiple_of((1 - c) * ROWS, 64)

    def clear(j, _):
        at = (lax.div(j, 16), lax.rem(lax.div(j, 4), 4), lax.rem(j, 4), pl.ds(spare, PAD - ROWS), slice(None))
        weights[at] = jnp.zeros((PAD - ROWS, LANE), BF)
        return 0

    lax.fori_loop(0, 64, clear, 0)
    for lo in range(2):
        load_cot(lo).wait()
        cot_t[lo, :, pl.ds(0, TOK)] = cot[lo, pl.ds(0, TOK), :].T
    pl.semaphore_wait(barrier, len(peers))

    def place(axis, by):
        return lax.rem(me[axis] + by + 4, 4)

    def pair(half):
        return pl.ds(2 * half, 2)

    every = slice(None)

    class Gather:
        def __init__(self, first, count, ring, turn_axis, half_axis, planes, base):
            self.first, self.count, self.ring = first, count, ring
            self.turn_axis, self.half_axis, self.planes = turn_axis, half_axis, planes
            self.base = base

        def at(self, spec, first, count):
            rows = pl.ds(pl.multiple_of(offset + first, 16), count)
            spec = {**{axis: me[axis] for axis in AXES}, **spec}
            return weights.at[spec["z"], spec["x"], spec["y"], rows, :]

        def sems(self, k):
            return ag_send.at[self.base + k], ag_recv.at[self.base + k]

        def first_start(self):
            for n, (first, count, one, two) in enumerate(self.planes):
                for by in FAR:
                    ref = self.at({}, first, count)
                    push(ref, ref, *self.sems(n * 6 + by - 1), device_at(moved(me, one, by)))

        def first_wait(self):
            for n, (first, count, one, two) in enumerate(self.planes):
                for by in FAR:
                    arrive(self.at({one: place(one, -by)}, first, count), *self.sems(n * 6 + by - 1))

        def second_start(self):
            for n, (first, count, one, two) in enumerate(self.planes):
                for by in FAR:
                    ref = self.at({one: every}, first, count)
                    push(ref, ref, *self.sems(n * 6 + 2 + by), device_at(moved(me, two, by)))

        def second_wait(self):
            for n, (first, count, one, two) in enumerate(self.planes):
                for by in FAR:
                    arrive(self.at({one: every, two: place(two, -by)}, first, count), *self.sems(n * 6 + 2 + by))

        def part(self, turn, half, where):
            spec = {
                self.turn_axis: place(self.turn_axis, GATHER_TURNS[turn]),
                self.half_axis: pair(half),
                self.ring: place(self.ring, where),
            }
            return self.at(spec, self.first, self.count)

        def ring_sems(self, turn, way, message):
            return self.sems(12 + turn * 6 + way * 3 + message)

        def start(self, turn):
            for message in range(2):
                for way in range(2):
                    ref = self.part(turn, message if way == 0 else 1 - message, 0)
                    push(ref, ref, *self.ring_sems(turn, way, message), device_at(moved(me, self.ring, 1 - 2 * way)))

        def forward(self, turn):
            for way in range(2):
                ref = self.part(turn, way, 2 * way - 1)
                arrive(ref, *self.ring_sems(turn, way, 0))
                push(ref, ref, *self.ring_sems(turn, way, 2), device_at(moved(me, self.ring, 1 - 2 * way)))

        def finish(self, turn):
            for way in range(2):
                arrive(self.part(turn, 1 - way, 2 * way - 1), *self.ring_sems(turn, way, 1))
                arrive(self.part(turn, way, 2), *self.ring_sems(turn, way, 2))

        def close(self):
            for n, (first, count, one, two) in enumerate(self.planes):
                for by in FAR:
                    left(self.at({}, first, count), *self.sems(n * 6 + by - 1))
                    left(self.at({one: every}, first, count), *self.sems(n * 6 + 2 + by))
            for turn in range(4):
                for k in range(6):
                    left(self.part(turn, 0, 0), *self.sems(12 + turn * 6 + k))

    ag = [Gather(*part, p * 36) for p, part in enumerate(GATHER_PARTS)]
    ag_z, ag_x, ag_y = ag

    class Copies:
        def __init__(self, order, first, count, z_half, base):
            self.one, self.two = order
            self.first, self.count, self.z_half, self.base = first, count, z_half, base

        def at(self, one, two, half=None):
            spec = {self.one: one, self.two: two}
            rows = pl.ds(self.first, self.count)
            if half is not None:
                rows = pl.ds(self.first + half * self.count // 2, self.count // 2)
            return copies.at[self.z_half, spec["x"], spec["y"], rows, :]

        def sems(self, k):
            return nc_send.at[self.base + k], nc_recv.at[self.base + k]

        def first_start(self):
            ref = self.at(me[self.one], me[self.two])
            for by in FAR:
                push(ref, ref, *self.sems(by - 1), device_at(moved(me, self.one, by)))

        def first_wait(self, by):
            arrive(self.at(place(self.one, -by), me[self.two]), *self.sems(by - 1))

        def part(self, by, half, where):
            return self.at(place(self.one, by), place(self.two, where), half)

        def ring_sems(self, by, way, message):
            return self.sems(3 + by * 6 + way * 3 + message)

        def start(self, by):
            for message in range(2):
                for way in range(2):
                    ref = self.part(by, message if way == 0 else 1 - message, 0)
                    push(ref, ref, *self.ring_sems(by, way, message), device_at(moved(me, self.two, 1 - 2 * way)))

        def forward(self, by):
            for way in range(2):
                ref = self.part(by, way, 2 * way - 1)
                arrive(ref, *self.ring_sems(by, way, 0))
                push(ref, ref, *self.ring_sems(by, way, 2), device_at(moved(me, self.two, 1 - 2 * way)))

        def finish(self, by):
            for way in range(2):
                arrive(self.part(by, 1 - way, 2 * way - 1), *self.ring_sems(by, way, 1))
                arrive(self.part(by, way, 2), *self.ring_sems(by, way, 2))

        def close(self):
            for by in FAR:
                left(self.at(me[self.one], me[self.two]), *self.sems(by - 1))
            for by in range(4):
                for k in range(6):
                    left(self.part(by, 0, 0), *self.sems(3 + by * 6 + k))

    nc = [
        [
            Copies(order, first, count, z_half, 2 + (g * 2 + p) * 27)
            for p, (first, count, order) in enumerate(COPY_PARTS)
        ]
        for g, z_half in enumerate((z_hi, 1 - z_hi))
    ]

    class Reduce:
        def __init__(self, order, first, count, got, base):
            self.one, self.two, self.three = order
            self.rows = pl.ds(first, count)
            self.got1, self.got2, self.got3 = got
            self.base = base

        def index(self, one, two, three):
            spec = {self.one: one, self.two: two, self.three: three}
            return spec["z"], spec["x"], spec["y"], self.rows, every

        def sems(self, k):
            return rs_send.at[self.base + k], rs_recv.at[self.base + k]

        def ring_index(self, turn, where, half):
            return self.index(place(self.one, where), place(self.two, REDUCE_TURNS[turn]), pair(half))

        def out(self, turn, where, half, slot, way):
            push(
                terms.at[self.ring_index(turn, where, half)], self.got1.at[turn, slot],
                *self.sems(turn * 6 + slot), device_at(moved(me, self.one, 1 - 2 * way)),
            )

        def far(self, turn):
            self.out(turn, 2, 0, 0, 0)
            self.out(turn, 2, 1, 1, 1)

        def near(self, turn, way):
            if way == 0:
                self.out(turn, 1, 1, 3, 0)
            else:
                self.out(turn, -1, 0, 5, 1)

        def combine(self, turn):
            for way in range(2):
                arrive(self.got1.at[turn, way], *self.sems(turn * 6 + way))
                at = self.ring_index(turn, 1 - 2 * way, way)
                total = terms[at].astype(F32) + self.got1[turn, way].astype(F32)
                terms[at] = total.astype(BF)
                self.out(turn, 1 - 2 * way, way, 2 if way == 0 else 4, way)

        def line(self, by):
            return self.index(me[self.one], place(self.two, by), every)

        def finish(self, turn):
            for half, (one, two) in enumerate(((2, 5), (3, 4))):
                arrive(self.got1.at[turn, one], *self.sems(turn * 6 + one))
                arrive(self.got1.at[turn, two], *self.sems(turn * 6 + two))
                at = self.ring_index(turn, 0, half)
                total = (
                    terms[at].astype(F32)
                    + self.got1[turn, one].astype(F32)
                    + self.got1[turn, two].astype(F32)
                )
                terms[at] = total.astype(BF)
            by = REDUCE_TURNS[turn]
            if by:
                push(
                    terms.at[self.line(by)], self.got2.at[by - 1],
                    *self.sems(23 + by), device_at(moved(me, self.two, by)),
                )

        def second(self):
            for by in FAR:
                arrive(self.got2.at[by - 1], *self.sems(23 + by))
            total = terms[self.line(0)].astype(F32)
            for k in range(3):
                total += self.got2[k].astype(F32)
            terms[self.line(0)] = total.astype(BF)
            for by in FAR:
                push(
                    terms.at[self.index(me[self.one], me[self.two], place(self.three, by))],
                    self.got3.at[by - 1], *self.sems(26 + by), device_at(moved(me, self.three, by)),
                )

        def third(self):
            for by in FAR:
                arrive(self.got3.at[by - 1], *self.sems(26 + by))
            total = terms[self.index(me[self.one], me[self.two], me[self.three])].astype(F32)
            for k in range(3):
                total += self.got3[k].astype(F32)
            grad_sum[self.rows, :] = total

        def close(self):
            for turn in range(4):
                for slot in range(6):
                    left(self.got1.at[turn, slot], *self.sems(turn * 6 + slot))
            for by in FAR:
                left(self.got2.at[by - 1], *self.sems(23 + by))
                left(self.got3.at[by - 1], *self.sems(26 + by))

    got = ((got1a, got2a, got3a), (got1b, got2b, got3b), (got1c, got2c, got3c))
    rs = [
        Reduce(order, first, count, got[p], p * 30)
        for p, (first, count, order) in enumerate(REDUCE_PARTS)
    ]
    rs_z, rs_x, rs_y = rs

    for lo in range(2):
        push(
            cotangent.at[:, pl.ds(sib_window[lo], PAD)], cot.at[lo, pl.ds(TOK, TOK)],
            core_send.at[lo], core_recv.at[lo], sibling,
        )
    for i in range(N_CHUNK):
        hi, x = term_chunk(i)
        q = hi * 4 + x
        push(
            tokens.at[:, columns(q)], tok.at[q, pl.ds(TOK, TOK)],
            core_send.at[2 + i], core_recv.at[2 + i], sibling,
        )

    load_state(0).wait()
    weights[me["z"], me["x"], me["y"], pl.ds(pl.multiple_of(offset, 32), ROWS), :] = state[0].astype(BF)
    for part in ag:
        part.first_start()
    for lo in range(2):
        arrive(cot.at[lo, pl.ds(TOK, TOK)], core_send.at[lo], core_recv.at[lo])
        cot_t[lo, :, pl.ds(TOK, TOK)] = cot[lo, pl.ds(TOK, TOK), :].T

    for part in ag:
        part.first_wait()
        part.second_start()

    def send_turn(parts, turn):
        for part in parts:
            part.far(turn)
            for way in range(2):
                part.near(turn, way)

    def term(i, _):
        hi, x = term_chunk(i)
        q = hi * 4 + x
        load_tok(i).wait()
        arrive(tok.at[q, pl.ds(TOK, TOK)], core_send.at[2 + i], core_recv.at[2 + i])
        for lo in range(2):
            part = jnp.dot(
                cot_t[lo, pl.ds(pl.multiple_of(offset, 64), ROWS), :], tok[q],
                preferred_element_type=F32,
            ).astype(BF)
            for y in range(4):
                terms[hi * 2 + lo, x, y] = part[:, y * LANE:(y + 1) * LANE]

        @pl.when(i == 1)
        def _():
            send_turn((rs_z,), 0)
            for turn in range(2):
                rs_x.far(turn)

        @pl.when(i == 3)
        def _():
            send_turn((rs_z,), 1)
            for turn in range(2):
                rs_x.near(turn, 0)

        @pl.when(i == 5)
        def _():
            for turn in range(2):
                rs_x.near(turn, 1)

        return 0

    lax.fori_loop(0, N_CHUNK, term, 0)

    def gather(action, *args):
        for part in ag:
            getattr(part, action)(*args)

    def reduce(action, *args):
        for part in rs:
            getattr(part, action)(*args)

    first = (rs_z, rs_x)

    def both(action, turn):
        for part in first:
            getattr(part, action)(turn)

    send_turn((rs_y,), 0)
    send_turn((rs_y,), 1)
    both("combine", 0)
    send_turn(first, 2)
    both("combine", 1)
    rs_y.combine(0)
    reduce("finish", 0)
    send_turn(rs, 3)
    send_turn((rs_y,), 2)
    rs_y.combine(1)
    both("combine", 2)
    reduce("finish", 1)
    gather("second_wait")
    rs_y.combine(2)
    both("combine", 3)
    reduce("finish", 2)
    rs_y.combine(3)
    gather("start", 0)
    ag_x.start(1)
    reduce("finish", 3)
    gather("forward", 0)
    ag_x.forward(1)
    reduce("second")
    ag_z.start(1)
    ag_x.start(2)
    ag_x.start(3)
    reduce("third")

    def update():
        load_state(1).wait()
        load_state(2).wait()
        grad = grad_sum[...] / math.sqrt(TOK * 128)
        one = beta_one * state[1] + (1.0 - beta_one) * grad
        two = beta_two * state[2] + (1.0 - beta_two) * grad * grad
        first_fix = 1.0 - beta_one**step_count
        second_fix = 1.0 - beta_two**step_count
        step = one / first_fix / (jnp.sqrt(two / second_fix) + epsilon)
        moved_master = state[0] - step_size * (step + decay_rate * state[0])
        state_new[0] = moved_master
        state_new[1] = one
        state_new[2] = two
        copies[z_hi, me["x"], me["y"]] = moved_master.astype(BF)
        for p, (first, count, _) in enumerate(COPY_PARTS):
            ref = copies.at[z_hi, me["x"], me["y"], pl.ds(first, count)]
            push(ref, ref, nc_send.at[p], nc_recv.at[p], opposite_z)
        for part in nc[0]:
            part.first_start()
            part.start(0)

    def copies_rest(g):
        def run():
            for by in FAR:
                for part in nc[g]:
                    part.first_wait(by)
                    part.start(4 - by)
        return run

    def copies_other():
        for p, (first, count, _) in enumerate(COPY_PARTS):
            arrive(
                copies.at[1 - z_hi, me["x"], me["y"], pl.ds(first, count)],
                nc_send.at[p], nc_recv.at[p],
            )
        for part in nc[1]:
            part.first_start()
            part.start(0)

    def copies_forward(g, *turns):
        def run():
            for by in turns:
                for part in nc[g]:
                    part.forward(by)
        return run

    def after_pass(step):
        if step == 0:
            copies_rest(0)()
            ag_x.forward(2)
            ag_x.forward(3)
            ag_z.forward(1)
            ag_y.forward(1)
        if step == 1:
            copies_other()
            ag_z.start(2)
            ag_y.start(2)
        if step == 2:
            copies_rest(1)()
            copies_forward(0, 0)()
            for turn in (1, 2, 3):
                ag_x.finish(turn)
            ag_z.finish(1)
            ag_y.finish(1)
        if step == 3:
            copies_forward(0, 3)()
            ag_z.forward(2)
            ag_y.forward(2)
        if step == 4:
            copies_forward(0, 1)()
            copies_forward(1, 0)()
            ag_z.start(3)
            ag_y.start(3)
        if step == 5:
            copies_forward(0, 2)()
            ag_z.finish(2)
            ag_y.finish(2)
        if step == 6:
            ag_z.forward(3)
            ag_y.forward(3)
            copies_forward(1, 3)()
        if step == 7:
            copies_forward(1, 1)()
        if step == 8:
            copies_forward(1, 2)()
            ag_z.finish(3)
            ag_y.finish(3)

    update()
    ag_y.start(1)
    reduce("close")
    gather("finish", 0)

    inv_width = 1.0 / math.sqrt(4096)
    inv_hidden = 1.0 / math.sqrt(1792)

    def ig_chunk(i):
        hi, x = pass_chunk(i)
        return hi * 4 + x

    def close_ig(i):
        q = ig_chunk(i)
        arrive(ig_recv.at[q], core_send.at[10 + i], core_recv.at[10 + i])
        total = ig_own[lax.rem(i, 2)] + ig_recv[q].astype(F32)
        ig_recv[q] = (total * inv_hidden).astype(BF)

    def against(j, _):
        chunks = [pass_chunk(2 * j + k) for k in range(2)]
        block = [
            [
                jnp.concatenate([weights[hi * 2 + lo, x, y] for y in range(4)], axis=1)
                for lo in range(2)
            ]
            for hi, x in chunks
        ]

        def events(k):
            for pair_at in range(4):
                if 3 * pair_at + k < 9:
                    pl.when(j == pair_at)(lambda step=3 * pair_at + k: after_pass(step))

        for k, (hi, x) in enumerate(chunks):
            q = hi * 4 + x
            i = 2 * j + k

            def backward(first):
                return sum(
                    jnp.dot(cot[lo, pl.ds(first, TOK), :], block[k][lo], preferred_element_type=F32)
                    for lo in range(2)
                )

            ig_send[i] = backward(TOK).astype(BF)
            push(ig_send.at[i], ig_recv.at[q], core_send.at[10 + i], core_recv.at[10 + i], sibling)
            ig_own[k] = backward(0)
            if k:
                close_ig(i - 1)
            else:

                @pl.when(j > 0)
                def _():
                    close_ig(i - 1)

            events(k)

        both = jnp.concatenate([tok[hi * 4 + x] for hi, x in chunks], axis=1)
        for lo in range(2):
            forward = lax.dot_general(
                both, jnp.concatenate([block[k][lo] for k in range(2)], axis=1),
                (((1,), (1,)), ((), ())), preferred_element_type=F32,
            )

            @pl.when(j == 0)
            def _():
                out_acc[lo] = forward

            @pl.when(j > 0)
            def _():
                out_acc[lo] += forward

        events(2)
        return 0

    lax.fori_loop(0, N_CHUNK // 2, against, 0)

    for lo in range(2):
        out_send[lo] = (out_acc[lo, pl.ds(TOK, TOK), :] * inv_width).astype(BF)
        push(out_send.at[lo], out_recv.at[lo], core_send.at[18 + lo], core_recv.at[18 + lo], sibling)
    close_ig(N_CHUNK - 1)

    for lo in range(2):
        arrive(out_recv.at[lo], core_send.at[18 + lo], core_recv.at[18 + lo])
        own = (out_acc[lo, pl.ds(0, TOK), :] * inv_width).astype(BF)
        theirs = out_recv[lo]

        def write(low, high, lo=lo):
            base = lo * 896
            out_full[:, base:base + 384] = low[:, :384]
            out_full[:, base + 384:base + 512] = low[:, 384:] + high[:, :128]
            out_full[:, base + 512:base + 896] = high[:, 128:]

        @pl.when(c == 0)
        def _():
            write(own, theirs)

        @pl.when(c == 1)
        def _():
            write(theirs, own)

    gather("close")
    for g in range(2):
        for by in range(4):
            for part in nc[g]:
                part.finish(by)

    for p, (first, count, _) in enumerate(COPY_PARTS):
        left(
            copies.at[z_hi, me["x"], me["y"], pl.ds(first, count)], nc_send.at[p], nc_recv.at[p]
        )
        for g in range(2):
            nc[g][p].close()
    for lo in range(2):
        left(cot.at[lo, pl.ds(TOK, TOK)], core_send.at[lo], core_recv.at[lo])
        left(out_send.at[lo], core_send.at[18 + lo], core_recv.at[18 + lo])
    for i in range(N_CHUNK):
        left(tok.at[0, pl.ds(TOK, TOK)], core_send.at[2 + i], core_recv.at[2 + i])
        left(ig_send.at[i], core_send.at[10 + i], core_recv.at[10 + i])


def local(tokens, cotangent, master, moment_one, moment_two):
    vmem = pltpu.VMEM
    dma = pltpu.SemaphoreType.DMA
    hidden = cotangent.shape[1]
    width = tokens.shape[1]
    anywhere = pl.BlockSpec(memory_space=pl.ANY)
    state_shape = jax.ShapeDtypeStruct((ROWS, LANE), F32)
    got = []
    for _, count, _ in REDUCE_PARTS:
        got.append(vmem((4, 6, 2, count, LANE), BF))
    for _, count, _ in REDUCE_PARTS:
        got.append(vmem((3, 4, count, LANE), BF))
    for _, count, _ in REDUCE_PARTS:
        got.append(vmem((3, count, LANE), BF))
    inside = pl.BlockSpec(memory_space=vmem)
    held = pl.pallas_call(
        kernel,
        out_shape=(
            vmem((TOK, hidden), BF),
            vmem((N_CHUNK, TOK, CHUNK), BF),
            vmem((3, ROWS, LANE), F32),
            vmem((2, 4, 4, ROWS, LANE), BF),
        ),
        in_specs=[anywhere] * 5,
        out_specs=(inside,) * 4,
        scratch_shapes=[
            vmem((N_CHUNK, 2 * TOK, CHUNK), BF),
            vmem((2, 2 * TOK, PAD), BF),
            vmem((2, PAD, 2 * TOK), BF),
            vmem((4, 4, 4, PAD, LANE), BF),
            vmem((4, 4, 4, ROWS, LANE), BF),
            *got,
            vmem((ROWS, LANE), F32),
            vmem((2, 2 * TOK, PAD), F32),
            vmem((2, TOK, CHUNK), F32),
            vmem((N_CHUNK, TOK, CHUNK), BF),
            vmem((2, TOK, PAD), BF),
            vmem((2, TOK, PAD), BF),
            vmem((3, ROWS, LANE), F32),
            dma((5,)), dma((N_CHUNK,)),
            dma((20,)), dma((20,)), dma((108,)), dma((108,)), dma((90,)), dma((90,)),
            dma((110,)), dma((110,)),
        ],
        compiler_params=pltpu.CompilerParams(
            collective_id=0, has_side_effects=True, vmem_limit_bytes=54 * 2**20
        ),
        name="step",
    )(tokens, cotangent, master, moment_one, moment_two)
    return pl.pallas_call(
        store,
        out_shape=(
            jax.ShapeDtypeStruct((TOK, hidden), BF),
            jax.ShapeDtypeStruct((TOK, width), BF),
            state_shape, state_shape, state_shape,
            jax.ShapeDtypeStruct((ROWS, width), BF),
        ),
        in_specs=[anywhere] * 4,
        out_specs=(anywhere,) * 6,
        scratch_shapes=[dma((44,))],
        compiler_params=pltpu.CompilerParams(has_side_effects=True, vmem_limit_bytes=2**20),
        name="store",
    )(*held)


def store(
    out_full, ig_full, state_new, copies,
    outputs, input_grad, new_master, new_one, new_two, new_copy, sem,
):
    moves = [(out_full, outputs)]
    for q in range(N_CHUNK):
        moves.append((ig_full.at[q], input_grad.at[:, pl.ds(q * CHUNK, CHUNK)]))
    for k, ref in enumerate((new_master, new_one, new_two)):
        moves.append((state_new.at[k], ref))
    for b in range(32):
        moves.append((
            copies.at[b // 16, (b // 4) % 4, b % 4], new_copy.at[:, pl.ds(b * LANE, LANE)],
        ))
    pending = [pltpu.make_async_copy(src, dst, sem.at[k]) for k, (src, dst) in enumerate(moves)]
    for copy in pending:
        copy.start()
    for copy in pending:
        copy.wait()


def solution(mesh):
    placed = (
        P(("node", "dp"), None),
        P(("node", "dp"), None),
        P("node", "dp"),
        P("node", "dp"),
        P("node", "dp"),
    )
    return jax.shard_map(
        local,
        mesh=mesh,
        in_specs=placed,
        out_specs=(
            P(("node", "dp"), None),
            P(("node", "dp"), None),
            P("node", "dp"),
            P("node", "dp"),
            P("node", "dp"),
            P("node", None),
        ),
        check_vma=False,
    )
```
